32 devices in a mesh: groups: 2 (over x), tensor: 4 (over y, core), adapter: 4 (over z).
Axes of the slice: x: 2, y: 2, z: 4, core: 2. Of those that a mesh axis runs over, the one named last changes fastest.
Arguments:
- tokens: bfloat16 [2048, 8192], P(('groups', 'adapter'), 'tensor'), parts along dimension 0, may hold values from -6 to 6
- tenant: int32 [2048, 1], P(('groups', 'adapter')), parts along dimension 0, may hold values from 0 to 7; in each aligned block of 256 rows (0 to 255, 256 to 511, ...) at most 96 rows name the same one
- adapter_storage_rows: int32 [16], P('groups'), parts along dimension 0, may hold values from 0 to 7, each once
- frozen_projection_weight: bfloat16 [8192, 8192], P('tensor'), may hold values from -0.09375 to 0.09375
- shrink_factor_matrices: float32 [16, 64, 8192], P(('groups', 'adapter'), None, 'tensor'), parts along dimension 0, may hold values from -0.0625 to 0.0625
- expand_factor_matrices: float32 [16, 64, 8192], P(('groups', 'adapter'), None, 'tensor'), parts along dimension 0, may hold values from -0.0625 to 0.0625
- shrink_running_mean: float32 [16, 64, 8192], P(('groups', 'adapter'), None, 'tensor'), parts along dimension 0, may hold values from -6 to 6
- expand_running_mean: float32 [16, 64, 8192], P(('groups', 'adapter'), None, 'tensor'), parts along dimension 0, may hold values from -6 to 6
- shrink_running_variance: float32 [16, 64, 8192], P(('groups', 'adapter'), None, 'tensor'), parts along dimension 0, may hold values from 0.25 to 4
- expand_running_variance: float32 [16, 64, 8192], P(('groups', 'adapter'), None, 'tensor'), parts along dimension 0, may hold values from 0.25 to 4
- output_gradient: bfloat16 [2048, 8192], P(('groups', 'adapter'), 'tensor'), parts along dimension 0, may hold values from -6 to 6
Outputs:
- layer_result: bfloat16 [2048, 8192], P(('groups', 'adapter'), 'tensor'), parts along dimension 0
- input_sensitivity: bfloat16 [2048, 8192], P(('groups', 'adapter'), 'tensor'), parts along dimension 0
- revised_shrink_factor: float32 [16, 64, 8192], P(('groups', 'adapter'), None, 'tensor'), parts along dimension 0
- revised_expand_factor: float32 [16, 64, 8192], P(('groups', 'adapter'), None, 'tensor'), parts along dimension 0
- revised_shrink_mean: float32 [16, 64, 8192], P(('groups', 'adapter'), None, 'tensor'), parts along dimension 0
- revised_expand_mean: float32 [16, 64, 8192], P(('groups', 'adapter'), None, 'tensor'), parts along dimension 0
- revised_shrink_variance: float32 [16, 64, 8192], P(('groups', 'adapter'), None, 'tensor'), parts along dimension 0
- revised_expand_variance: float32 [16, 64, 8192], P(('groups', 'adapter'), None, 'tensor'), parts along dimension 0
The draws below stay inside these ranges and needn't reach their ends.
There are 2 independent parts, one for each index of `groups`. The reference program is written for one: setup_inputs(seed, part) draws one part's arguments, and reference() takes and returns one part's arrays. A program takes and returns all parts, laid end to end along the dimension named above; an argument that names none is the same for every part. Nothing has to cross between parts.
Inputs may be any that keep to these rules, and one draw needn't show every extreme that they name: `tenant`: among the 256 tokens of one index of adapter (aligned blocks of rows) no adapter id appears more than 96 times, and in at least one block some id appears exactly 96 times. `adapter_storage_rows`: A permutation: each storage row holds exactly one adapter.
All inputs are finite; a program needn't handle non-finite values.
Results may differ from the reference program's by a relative error of at most 0.013.
Values may be sent and summed in bfloat16 or wider, within the bound.
A program may use at most 192 MiB of HBM per device.

```python
import math
import jax
import jax.numpy as jnp
import numpy as np
from jax import lax

MODEL_WIDTH = 8192
ADAPTER_RANK = 64
TOK_DEV = 256
ADAPTER_TOTAL = 8
TOKENS = 1024
CAP = 96
N_ADAPTER = 4


def strengthened(result, own_key, source, target, parts, factor):
    def block_of(dim):
        return (jnp.arange(result.shape[dim]) // (result.shape[dim] // parts)).reshape((-1,) + (1,) * (result.ndim - 1 - dim))

    near = jax.random.permutation(own_key, parts)[block_of(target)]
    far = (block_of(target) + parts // 2) % parts
    return jnp.where((block_of(source) == near) | (block_of(source) == far), factor * result, result)


def shard_levels(own_key, extent, cuts, low, largest):
    factor_of, own = 1.0, jax.random.fold_in(own_key, 6)
    for dim, parts in cuts:
        draws = jnp.exp(jax.random.uniform(jax.random.fold_in(own, dim), (parts,), jnp.float32, low / len(cuts), largest / len(cuts)))
        factor_of = factor_of * jnp.repeat(draws, extent[dim] // parts).reshape([-1 if axis == dim else 1 for axis in range(len(extent))])
    return factor_of


def routed_block(own_key, own, number, rows, amount, top, most, slope):
    ranking = jax.random.permutation(own_key, amount)
    packed, usual = load_shares(amount, rows * top, most, slope, True), load_shares(amount, rows * top, most, slope, False)
    places = jnp.arange(amount)

    def named(sizes, rotation):
        used = int((sizes > 0).sum())
        fixed = max(1, used // 4)
        shifted = fixed + (places - fixed + rotation * (used - fixed)) % max(1, amount - fixed)
        return jnp.zeros((amount,), jnp.int32).at[ranking[jnp.where(places < fixed, places, shifted)]].set(jnp.asarray(sizes, jnp.int32))

    sizes = jnp.where(number % 4 == 0, named(packed, number // 4), named(usual, number - number // 4 - 1))
    mixed = jax.random.permutation(jax.random.fold_in(own, 3), amount)
    donor, receiver = mixed[0:amount // 2 * 2:2], mixed[1:amount // 2 * 2:2]
    room = jnp.minimum(sizes[donor] - 1, most - sizes[receiver]) // 2
    room = jnp.where((donor == ranking[0]) | (receiver == ranking[0]) | (sizes[receiver] == 0), 0, jnp.maximum(room, 0))
    shifted = jax.random.randint(jax.random.fold_in(own, 4), (amount // 2,), 0, 1 << 20) % (room + 1)
    sizes = sizes.at[donor].add(-shifted).at[receiver].add(shifted)
    members = jnp.searchsorted(jnp.cumsum(sizes), jnp.arange(rows * top), side="right").astype(jnp.int32)
    grid = members.reshape(top, rows).T
    grid = grid[jax.random.permutation(jax.random.fold_in(own, 1), rows)]
    rotation = jax.random.randint(jax.random.fold_in(own, 2), (rows, 1), 0, top)
    return jnp.take_along_axis(grid, (jnp.arange(top)[None, :] + rotation) % top, axis=1)


def load_shares(amount, total, bound, lean, full):
    portions = [(1 << 20) // math.isqrt(standing ** lean) + 1 for standing in range(1, amount + 1)]
    largest = bound if full else min(bound, max(-(-total // amount), total * portions[0] // sum(portions)))
    least = 1 if total - largest >= amount - 1 else 0
    counts, rest = [largest] + [least] * (amount - 1), total - largest - least * (amount - 1)
    while rest > 0:
        candidates = [i for i in range(1, amount) if counts[i] < largest] or [i for i in range(1, amount) if counts[i] < bound]
        pool, budget = sum([portions[i] for i in candidates]), rest
        for i in candidates:
            extra = min(bound - counts[i], max(1, budget * portions[i] // pool), rest)
            counts[i] = counts[i] + extra
            rest = rest - extra
    return np.array(counts)


def noise(stream_key, shape, spread, limit, shards=(), kind=jnp.bfloat16):
    factor_of = shard_levels(stream_key, shape, shards, -0.22, 0.18) if shards else 1.0
    result = jax.random.normal(stream_key, shape, jnp.float32) * spread * factor_of
    return jnp.minimum(jnp.maximum(result, -limit), limit).astype(kind)


def bell_draw_with(own_key, dims, deviation, reach, split, heavy, held_as=jnp.bfloat16):
    array = deviation * jax.random.normal(own_key, dims, jnp.float32)
    if split:
        array = array * shard_levels(own_key, dims, split, -0.22, 0.18)
    return jnp.clip(strengthened(array, jax.random.fold_in(own_key, 3), *heavy), -reach, reach).astype(held_as)


def setup_inputs(seed: int = 0, part: int = 0) -> dict:
    key_of = jax.random.split(jax.random.key(seed), 12)
    own_keys = jax.random.split(jax.random.fold_in(key_of[11], part), 12)
    tokens = noise(own_keys[0], (TOKENS, MODEL_WIDTH), 1.0, 6.0, ((0, 4), (1, 4)))
    tenant_keys = jax.random.split(jax.random.fold_in(own_keys[1], 1), TOKENS // TOK_DEV)
    tenant_turns = jax.random.permutation(jax.random.fold_in(own_keys[1], 3), TOKENS // TOK_DEV)
    tenant = jax.vmap(lambda own, number: routed_block(jax.random.fold_in(own_keys[1], 2), own, number, TOK_DEV, ADAPTER_TOTAL, 1, CAP, 2))(tenant_keys, tenant_turns).reshape((TOKENS, 1))
    adapter_storage_rows = jax.random.permutation(own_keys[2], ADAPTER_TOTAL).astype(jnp.int32)
    frozen_projection_weight = bell_draw_with(key_of[3], (MODEL_WIDTH, MODEL_WIDTH), MODEL_WIDTH ** -0.5, 0.09375, ((0, 4),), (0, 1, 4, 2.0))
    shrink_factor_matrices = noise(own_keys[4], (ADAPTER_TOTAL, ADAPTER_RANK, MODEL_WIDTH), MODEL_WIDTH ** -0.5, 0.0625, ((0, 4), (2, 4)), jnp.float32)
    expand_factor_matrices = noise(own_keys[5], (ADAPTER_TOTAL, ADAPTER_RANK, MODEL_WIDTH), MODEL_WIDTH ** -0.5, 0.0625, ((0, 4), (2, 4)), jnp.float32)
    shrink_running_mean = noise(own_keys[6], (ADAPTER_TOTAL, ADAPTER_RANK, MODEL_WIDTH), 1.0, 6.0, ((0, 4), (2, 4)), jnp.float32)
    expand_running_mean = noise(own_keys[7], (ADAPTER_TOTAL, ADAPTER_RANK, MODEL_WIDTH), 1.0, 6.0, ((0, 4), (2, 4)), jnp.float32)
    shrink_running_variance = jnp.clip(jnp.exp(math.log(4.0) - 2.7725887 * jax.random.uniform(own_keys[8], (ADAPTER_TOTAL, ADAPTER_RANK, MODEL_WIDTH), jnp.float32) ** shard_levels(own_keys[8], (ADAPTER_TOTAL, ADAPTER_RANK, MODEL_WIDTH), ((0, 4), (2, 4)), -0.2, 0.2)), 0.25, 4.0)
    expand_running_variance = jnp.clip(jnp.exp(math.log(4.0) - 2.7725887 * jax.random.uniform(own_keys[9], (ADAPTER_TOTAL, ADAPTER_RANK, MODEL_WIDTH), jnp.float32) ** shard_levels(own_keys[9], (ADAPTER_TOTAL, ADAPTER_RANK, MODEL_WIDTH), ((0, 4), (2, 4)), -0.2, 0.2)), 0.25, 4.0)
    output_gradient = noise(own_keys[10], (TOKENS, MODEL_WIDTH), 1.0, 6.0, ((0, 4), (1, 4)))
    return dict(tokens=tokens, tenant=tenant, adapter_storage_rows=adapter_storage_rows, frozen_projection_weight=frozen_projection_weight, shrink_factor_matrices=shrink_factor_matrices, expand_factor_matrices=expand_factor_matrices, shrink_running_mean=shrink_running_mean, expand_running_mean=expand_running_mean, shrink_running_variance=shrink_running_variance, expand_running_variance=expand_running_variance, output_gradient=output_gradient)


beta_one = 0.9
beta_two = 0.999
learn_rate = 0.01
adam_eps = 1e-08
adam_step = 10
adapter_scale = 2.0

def optimizer_advance(param, grad, first, second):
    first_next = beta_one * first + (1.0 - beta_one) * grad
    second_next = beta_two * second + (1.0 - beta_two) * grad * grad
    fix_one = 1.0 - beta_one ** adam_step
    fix_two = 1.0 - beta_two ** adam_step
    param_next = param - learn_rate * (first_next / fix_one) / (jnp.sqrt(second_next / fix_two) + adam_eps)
    return (param_next, first_next, second_next)

def reference(tokens, tenant, adapter_storage_rows, frozen_projection_weight, shrink_factor_matrices, expand_factor_matrices, shrink_running_mean, expand_running_mean, shrink_running_variance, expand_running_variance, output_gradient):
    f32 = jnp.float32
    down_maps_half = shrink_factor_matrices.astype(jnp.bfloat16)
    up_maps_half = expand_factor_matrices.astype(jnp.bfloat16)
    stored = adapter_storage_rows[tenant[:, 0]].astype(jnp.int32)
    labels = jnp.arange(ADAPTER_TOTAL, dtype=jnp.int32)
    onehot = (stored[:, None] == labels[None, :]).astype(jnp.int32).reshape(N_ADAPTER, TOK_DEV, ADAPTER_TOTAL)
    before = jnp.cumsum(onehot, axis=1) - onehot
    rank_in = lax.optimization_barrier(jnp.sum(before * onehot, axis=2)).reshape(TOKENS).astype(jnp.int32)
    block = (jnp.arange(TOKENS, dtype=jnp.int32) // TOK_DEV).astype(jnp.int32)
    per_row = N_ADAPTER * CAP
    position = (stored * per_row + block * CAP + rank_in).astype(jnp.int32)
    total = ADAPTER_TOTAL * per_row
    source = jnp.zeros((total,), jnp.int32).at[position].set(jnp.arange(TOKENS, dtype=jnp.int32) + 1)
    filled = source > 0
    pick = jnp.maximum(source - 1, 0).astype(jnp.int32)
    x_slots = jnp.where(filled[:, None], tokens[pick], jnp.zeros((), jnp.bfloat16)).reshape(ADAPTER_TOTAL, per_row, MODEL_WIDTH)
    dy_slots = jnp.where(filled[:, None], output_gradient[pick], jnp.zeros((), jnp.bfloat16)).reshape(ADAPTER_TOTAL, per_row, MODEL_WIDTH)
    down32 = down_maps_half.astype(f32)
    up32 = up_maps_half.astype(f32)
    lowrank_activation = jnp.einsum('amd,ard->amr', x_slots.astype(f32), down32)
    lowrank_activation_half = (adapter_scale * lowrank_activation).astype(jnp.bfloat16)
    backward_lowrank = jnp.einsum('amd,ard->amr', dy_slots.astype(f32), up32)
    backward_lowrank_half = (adapter_scale * backward_lowrank).astype(jnp.bfloat16)
    delta = jnp.einsum('amr,ard->amd', lowrank_activation_half.astype(f32), up32).astype(jnp.bfloat16).reshape(total, MODEL_WIDTH)
    back = jnp.einsum('amr,ard->amd', backward_lowrank_half.astype(f32), down32).astype(jnp.bfloat16).reshape(total, MODEL_WIDTH)
    base = jnp.dot(tokens, frozen_projection_weight, preferred_element_type=f32)
    layer_result = (base + delta[position].astype(f32)).astype(jnp.bfloat16)
    base_back = lax.dot_general(output_gradient, frozen_projection_weight, (((1,), (1,)), ((), ())), preferred_element_type=f32)
    input_sensitivity = (base_back + back[position].astype(f32)).astype(jnp.bfloat16)
    shrink_factor_cotangent = jnp.einsum('amr,amd->ard', backward_lowrank_half.astype(f32), x_slots.astype(f32))
    expand_factor_cotangent = jnp.einsum('amr,amd->ard', lowrank_activation_half.astype(f32), dy_slots.astype(f32))
    revised_shrink_factor, revised_shrink_mean, revised_shrink_variance = optimizer_advance(shrink_factor_matrices, shrink_factor_cotangent, shrink_running_mean, shrink_running_variance)
    revised_expand_factor, revised_expand_mean, revised_expand_variance = optimizer_advance(expand_factor_matrices, expand_factor_cotangent, expand_running_mean, expand_running_variance)
    return (layer_result, input_sensitivity, revised_shrink_factor, revised_expand_factor, revised_shrink_mean, revised_expand_mean, revised_shrink_variance, revised_expand_variance)
```

```python
import jax
import jax.numpy as jnp
from jax import lax
from jax.sharding import PartitionSpec as P

beta_one = 0.9
beta_two = 0.999
learn_rate = 0.01
adam_eps = 1e-08
adam_step = 10
adapter_scale = 2.0
f32 = jnp.float32
half = jnp.bfloat16


def optimizer_advance(param, grad, first, second):
    first_next = beta_one * first + (1.0 - beta_one) * grad
    second_next = beta_two * second + (1.0 - beta_two) * grad * grad
    fix_one = 1.0 - beta_one**adam_step
    fix_two = 1.0 - beta_two**adam_step
    param_next = param - learn_rate * (first_next / fix_one) / (
        jnp.sqrt(second_next / fix_two) + adam_eps
    )
    return (param_next, first_next, second_next)


def swap(value, size, bit):
    return lax.ppermute(value, "tensor", [(i, i ^ bit) for i in range(size)])


def bits_down(size):
    bit = size // 2
    while bit:
        yield bit
        bit //= 2


def tensor_gather(value, size, me):
    rows, width = value.shape
    held = value[:, None, :]
    for bit in bits_down(size):
        other = swap(held, size, bit)
        high = (me & bit) != 0
        held = jnp.stack(
            [jnp.where(high, other, held), jnp.where(high, held, other)], axis=2
        ).reshape(rows, -1, width)
    return held.reshape(rows, size * width)


def tensor_scatter(value, size, me):
    rows = value.shape[0]
    held = value.reshape(rows, size, -1)
    width = held.shape[2]
    bit = 1
    total = held
    while bit < size:
        pairs = total.reshape(rows, -1, 2, width)
        mine = ((me & bit) != 0).astype(jnp.int32)
        keep = lax.dynamic_index_in_dim(pairs, mine, 2, keepdims=False)
        give = lax.dynamic_index_in_dim(pairs, 1 - mine, 2, keepdims=False)
        other = swap(give.astype(half), size, bit)
        total = keep.astype(f32) + other.astype(f32)
        bit *= 2
    return total.reshape(rows, width)


def tensor_sum(value, size):
    if size == 4:
        a, b, c = (swap(value, size, k) for k in (1, 2, 3))
        return (value + a) + (b + c)
    bit = 1
    while bit < size:
        value = value + swap(value, size, bit)
        bit *= 2
    return value


def chain_gather(own, size, me, after=None):
    left, right = [own], [own]
    for t in range(1, size):
        left.append(
            lax.ppermute(left[-1], "adapter", [(i, i + 1) for i in range(t - 1, size - 1)])
        )
        right.append(
            lax.ppermute(right[-1], "adapter", [(i, i - 1) for i in range(1, size - t + 1)])
        )
    slots = [own] + [jnp.where(me >= t, left[t], right[size - t]) for t in range(1, size)]
    return jnp.concatenate(slots, axis=0), left, right


def chain_scatter(terms, size):
    from_left = from_right = None
    for d in range(size - 1, 0, -1):
        rightward, leftward = terms[size - d], terms[d]
        if from_left is not None:
            rightward = rightward + from_left.astype(f32)
            leftward = leftward + from_right.astype(f32)
        from_left = lax.ppermute(
            rightward.astype(half), "adapter", [(i, i + 1) for i in range(size - d)]
        )
        from_right = lax.ppermute(
            leftward.astype(half), "adapter", [(i, i - 1) for i in range(d, size)]
        )
    total = terms[0]
    if from_left is not None:
        total = total + from_left.astype(f32) + from_right.astype(f32)
    return total


def make(n_tensor, n_adapter):
    def on_device(
        tokens,
        tenant,
        adapter_storage_rows,
        frozen_projection_weight,
        shrink_factor_matrices,
        expand_factor_matrices,
        shrink_running_mean,
        expand_running_mean,
        shrink_running_variance,
        expand_running_variance,
        output_gradient,
    ):
        count = adapter_storage_rows.shape[0]
        own, rank, width = shrink_factor_matrices.shape
        zi, ti = lax.axis_index("adapter"), lax.axis_index("tensor")
        down_own = shrink_factor_matrices.reshape(own * rank, width).astype(half)
        up_own = expand_factor_matrices.reshape(own * rank, width).astype(half)

        labels = lax.broadcasted_iota(jnp.int32, (1, count), 1)
        stored = jnp.sum(
            jnp.where(tenant == labels, adapter_storage_rows[None, :], 0), axis=1, keepdims=True
        )
        place = lax.broadcasted_iota(jnp.int32, (1, count * rank), 1) // rank
        row_of = lax.rem(zi - place // own + n_adapter, n_adapter) * own + lax.rem(place, own)
        mask = stored == row_of

        def fold(values):
            values = jnp.where(mask, values, 0.0)
            return sum(values[:, a * rank : (a + 1) * rank] for a in range(count))

        def spread(low):
            return jnp.where(mask, jnp.tile(low, (1, count)), jnp.zeros((), low.dtype))

        def last(a, b):
            return lax.dot_general(a, b, (((1,), (1,)), ((), ())), preferred_element_type=f32)

        down_all, _, _ = chain_gather(down_own, n_adapter, zi)
        up_all, _, _ = chain_gather(up_own, n_adapter, zi)

        partial = jnp.dot(
            tokens, frozen_projection_weight, preferred_element_type=f32
        ).astype(half)
        base_out = tensor_scatter(partial, n_tensor, ti)
        dy_full = tensor_gather(output_gradient, n_tensor, ti)

        def blocks(terms):
            return list(terms.reshape(n_adapter, own * rank, width))

        low = tensor_sum(fold(last(tokens, down_all)), n_tensor)
        low = spread((adapter_scale * low).astype(half))
        terms_up = lax.dot_general(
            low, output_gradient, (((0,), (0,)), ((), ())), preferred_element_type=f32
        )
        grad_up = chain_scatter(blocks(terms_up), n_adapter)

        back_low = tensor_sum(fold(last(output_gradient, up_all)), n_tensor)
        back_low = spread((adapter_scale * back_low).astype(half))
        terms_down = lax.dot_general(
            back_low, tokens, (((0,), (0,)), ((), ())), preferred_element_type=f32
        )
        grad_down = chain_scatter(blocks(terms_down), n_adapter)

        delta = jnp.dot(low, up_all, preferred_element_type=f32).astype(half)
        back = jnp.dot(back_low, down_all, preferred_element_type=f32).astype(half)
        layer_result = (base_out + delta.astype(f32)).astype(half)
        base_back = last(dy_full, frozen_projection_weight)
        input_sensitivity = (base_back + back.astype(f32)).astype(half)

        shape = shrink_factor_matrices.shape
        p_up, m_up, v_up = optimizer_advance(
            expand_factor_matrices,
            grad_up.reshape(shape),
            expand_running_mean,
            expand_running_variance,
        )
        p_down, m_down, v_down = optimizer_advance(
            shrink_factor_matrices,
            grad_down.reshape(shape),
            shrink_running_mean,
            shrink_running_variance,
        )
        return (layer_result, input_sensitivity, p_down, p_up, m_down, m_up, v_down, v_up)

    return on_device


def solution(mesh):
    rows = P(("groups", "adapter"), "tensor")
    maps = P(("groups", "adapter"), None, "tensor")
    return jax.shard_map(
        make(mesh.shape["tensor"], mesh.shape["adapter"]),
        mesh=mesh,
        in_specs=(rows, P(("groups", "adapter"), None), P("groups"), P("tensor", None))
        + (maps,) * 6
        + (rows,),
        out_specs=(rows, rows) + (maps,) * 6,
        check_vma=False,
    )
```

```python
import jax
import jax.numpy as jnp
from jax import lax
from jax.experimental import pallas as pl
from jax.experimental.pallas import tpu as pltpu
from jax.sharding import PartitionSpec as P

beta_one = 0.9
beta_two = 0.999
learn_rate = 0.01
adam_eps = 1e-08
adam_step = 10
adapter_scale = 2.0
f32 = jnp.float32
half = jnp.bfloat16


def optimizer_advance(param, grad, first, second):
    first_next = beta_one * first + (1.0 - beta_one) * grad
    second_next = beta_two * second + (1.0 - beta_two) * grad * grad
    fix_one = 1.0 - beta_one**adam_step
    fix_two = 1.0 - beta_two**adam_step
    param_next = param - learn_rate * (first_next / fix_one) / (
        jnp.sqrt(second_next / fix_two) + adam_eps
    )
    return (param_next, first_next, second_next)


def swap(value, size, bit):
    return lax.ppermute(value, "tensor", [(i, i ^ bit) for i in range(size)])


def bits_down(size):
    bit = size // 2
    while bit:
        yield bit
        bit //= 2


def tensor_gather(value, size, me):
    rows, width = value.shape
    held = value[:, None, :]
    for bit in bits_down(size):
        other = swap(held, size, bit)
        high = (me & bit) != 0
        held = jnp.stack(
            [jnp.where(high, other, held), jnp.where(high, held, other)], axis=2
        ).reshape(rows, -1, width)
    return held.reshape(rows, size * width)


def tensor_scatter(value, size, me):
    rows = value.shape[0]
    held = value.reshape(rows, size, -1)
    width = held.shape[2]
    bit = 1
    total = held
    while bit < size:
        pairs = total.reshape(rows, -1, 2, width)
        mine = ((me & bit) != 0).astype(jnp.int32)
        keep = lax.dynamic_index_in_dim(pairs, mine, 2, keepdims=False)
        give = lax.dynamic_index_in_dim(pairs, 1 - mine, 2, keepdims=False)
        other = swap(give.astype(half), size, bit)
        total = keep.astype(f32) + other.astype(f32)
        bit *= 2
    return total.reshape(rows, width)


def tensor_sum(value, size):
    if size == 4:
        a, b, c = (swap(value, size, k) for k in (1, 2, 3))
        return (value + a) + (b + c)
    bit = 1
    while bit < size:
        value = value + swap(value, size, bit)
        bit *= 2
    return value


def chain_gather(own, size, me, after=None):
    left, right = [own], [own]
    for t in range(1, size):
        left.append(
            lax.ppermute(left[-1], "adapter", [(i, i + 1) for i in range(t - 1, size - 1)])
        )
        right.append(
            lax.ppermute(right[-1], "adapter", [(i, i - 1) for i in range(1, size - t + 1)])
        )
    slots = [own] + [jnp.where(me >= t, left[t], right[size - t]) for t in range(1, size)]
    return jnp.concatenate(slots, axis=0), left, right


def chain_scatter(terms, size):
    from_left = from_right = None
    for d in range(size - 1, 0, -1):
        rightward, leftward = terms[size - d], terms[d]
        if from_left is not None:
            rightward = rightward + from_left.astype(f32)
            leftward = leftward + from_right.astype(f32)
        from_left = lax.ppermute(
            rightward.astype(half), "adapter", [(i, i + 1) for i in range(size - d)]
        )
        from_right = lax.ppermute(
            leftward.astype(half), "adapter", [(i, i - 1) for i in range(d, size)]
        )
    total = terms[0]
    if from_left is not None:
        total = total + from_left.astype(f32) + from_right.astype(f32)
    return total


TILE = 512
MESH = pl.DeviceIdType.MESH


def dot_last(a, b):
    return lax.dot_general(a, b, (((1,), (1,)), ((), ())), preferred_element_type=f32)


def dot_first(a, b):
    return lax.dot_general(a, b, (((0,), (0,)), ((), ())), preferred_element_type=f32)


def fused_kernel(
    x, dy, mask, down, up, w,
    layer, sens, grad_down, grad_up,
    g_down, g_up, t_down, t_up, r_down, r_up,
    part, near, far, dyg, acc, lows, low_in, spread_low,
    wbuf, w_sem, z_send, z_recv, r_send, r_recv, y_send, y_recv, l_send, l_recv,
):
    zi, ti = lax.axis_index("adapter"), lax.axis_index("tensor")
    nz = 4
    peers = [ti, ti + 1 - 2 * (ti % 2), (ti + 2) % 4, 3 - ti]
    width = x.shape[1]
    tiles = width // TILE

    def when(cond, fn):
        pl.when(cond)(fn)

    barrier = pltpu.get_barrier_semaphore()
    when(zi > 0, lambda: pl.semaphore_signal(
        barrier, inc=1, device_id={"adapter": zi - 1}, device_id_type=MESH))
    when(zi < nz - 1, lambda: pl.semaphore_signal(
        barrier, inc=1, device_id={"adapter": zi + 1}, device_id_type=MESH))
    for k in (1, 2, 3):
        pl.semaphore_signal(barrier, inc=1, device_id={"tensor": peers[k]}, device_id_type=MESH)
    g_down[zi] = down[...].astype(half)
    g_up[zi] = up[...].astype(half)

    order = [3, 2, 1, 0, 0, 1, 2, 3]

    def w_copy(s, j, slot):
        column = pl.multiple_of(peers[order[s]] * width + j * TILE, TILE)
        return pltpu.make_async_copy(w.at[:, pl.ds(column, TILE)], wbuf.at[slot], w_sem.at[slot])

    w_copy(0, 0, 0).start()
    inside = (zi > 0) & (zi < nz - 1)
    when(inside, lambda: pl.semaphore_wait(barrier, 5))
    when(jnp.logical_not(inside), lambda: pl.semaphore_wait(barrier, 4))

    def remote_z(src, dst, send, recv, direction):
        to = zi + 1 if direction == 0 else zi - 1
        return pltpu.make_async_remote_copy(
            src_ref=src, dst_ref=dst, send_sem=send, recv_sem=recv,
            device_id={"adapter": to}, device_id_type=MESH)

    def gather_copy(kind, t, direction, owner):
        g = (g_down, g_up)[kind]
        return remote_z(g.at[owner], g.at[owner], z_send.at[kind, direction, t - 1],
                        z_recv.at[kind, direction, t - 1], direction)

    def may_right(t):
        return (zi < nz - 1) & (zi - t + 1 >= 0)

    def may_left(t):
        return (zi > 0) & (zi + t - 1 <= nz - 1)

    def hop(kind, t):
        when(may_right(t), lambda: gather_copy(kind, t, 0, zi - t + 1).start())
        when(may_left(t), lambda: gather_copy(kind, t, 1, zi + t - 1).start())

    def land(kind, t):
        when(zi - t >= 0, lambda: gather_copy(kind, t, 0, zi - t).wait_recv())
        when(zi + t <= nz - 1, lambda: gather_copy(kind, t, 1, zi + t).wait_recv())

    def sent(kind, t):
        when(may_right(t), lambda: gather_copy(kind, t, 0, zi - t + 1).wait_send())
        when(may_left(t), lambda: gather_copy(kind, t, 1, zi + t - 1).wait_send())

    def reduce_copy(kind, d, direction, owner):
        terms, arrived = ((t_down, r_down), (t_up, r_up))[kind]
        return remote_z(terms.at[owner], arrived.at[direction, d - 1],
                        r_send.at[kind, direction, d - 1], r_recv.at[kind, direction, d - 1],
                        direction)

    def reduce_hop(kind, d):
        terms, arrived = ((t_down, r_down), (t_up, r_up))[kind]

        def go(direction):
            owner = zi + d if direction == 0 else zi - d

            def fn():
                if d < nz - 1:
                    def add():
                        terms[owner] = (
                            terms[owner].astype(f32) + arrived[direction, d].astype(f32)
                        ).astype(half)

                    when(zi > 0 if direction == 0 else zi < nz - 1, add)
                reduce_copy(kind, d, direction, owner).start()

            return fn

        when(zi + d <= nz - 1, go(0))
        when(zi - d >= 0, go(1))

    def reduce_land(kind, d):
        when((zi > 0) & (zi - 1 + d <= nz - 1),
             lambda: reduce_copy(kind, d, 0, 0).wait_recv())
        when((zi < nz - 1) & (zi + 1 - d >= 0),
             lambda: reduce_copy(kind, d, 1, 0).wait_recv())

    def reduce_sent(kind, d):
        when(zi + d <= nz - 1, lambda: reduce_copy(kind, d, 0, zi + d).wait_send())
        when(zi - d >= 0, lambda: reduce_copy(kind, d, 1, zi - d).wait_send())

    def reduce_end(kind, out):
        terms, arrived = ((t_down, r_down), (t_up, r_up))[kind]
        out[...] = terms[zi].astype(f32)

        def add(direction):
            def fn():
                out[...] += arrived[direction, 0].astype(f32)
            return fn

        when(zi > 0, add(0))
        when(zi < nz - 1, add(1))

    def remote_y(src, dst, n, k):
        return pltpu.make_async_remote_copy(
            src_ref=src, dst_ref=dst, send_sem=y_send.at[n], recv_sem=y_recv.at[n],
            device_id={"tensor": peers[k]}, device_id_type=MESH)

    dy_far = remote_y(dy, dyg.at[1], 0, 2)
    dy_near = remote_y(dy, dyg.at[0], 1, 1)
    dy_relay = remote_y(dyg.at[1], dyg.at[2], 2, 1)
    near_first = remote_y(part.at[3], near.at[0], 3, 1)
    near_second = remote_y(part.at[1], near.at[1], 4, 1)
    far_copy = remote_y(part.at[2], far, 5, 2)

    def stream(s, use):
        def step(j, carry):
            slot = lax.rem(j, 2)
            w_copy(s, j, slot).wait()

            @pl.when(j < tiles - 1)
            def _():
                w_copy(s, j + 1, 1 - slot).start()

            if s + 1 < len(order):
                @pl.when(j == tiles - 1)
                def _():
                    w_copy(s + 1, 0, 1 - slot).start()

            use(pl.ds(pl.multiple_of(j * TILE, TILE), TILE), wbuf.at[slot])
            return carry

        lax.fori_loop(0, tiles, step, 0)

    def forward(s):
        def use(columns, tile):
            part[order[s], :, columns] = jnp.dot(
                x[...], tile[...], preferred_element_type=f32
            ).astype(half)
        stream(s, use)

    def backward(s):
        k = order[s]
        source = dy if k == 0 else dyg.at[k - 1]

        def use(columns, tile):
            acc[...] += dot_last(source[:, columns], tile[...])
        stream(s, use)

    def low_start(kind, tokens, maps):
        total = jnp.zeros((x.shape[0], 128), f32)
        for o in range(nz):
            product = dot_last(tokens[...], maps[o])
            total += jnp.where(mask[:, o * 128:(o + 1) * 128] > 0.5, product, 0.0)
        lows[kind] = total
        for k in (1, 2, 3):
            low_copy(kind, k).start()

    def low_copy(kind, k):
        return pltpu.make_async_remote_copy(
            src_ref=lows.at[kind], dst_ref=low_in.at[kind, k - 1],
            send_sem=l_send.at[kind, k - 1], recv_sem=l_recv.at[kind, k - 1],
            device_id={"tensor": peers[k]}, device_id_type=MESH)

    def low_end(kind, tokens, terms):
        for k in (1, 2, 3):
            low_copy(kind, k).wait_recv()
        total = (lows[kind] + low_in[kind, 0]) + (low_in[kind, 1] + low_in[kind, 2])
        value = adapter_scale * total
        for o in range(nz):
            block = jnp.where(mask[:, o * 128:(o + 1) * 128] > 0.5, value, 0.0).astype(half)
            spread_low[kind, :, o * 128:(o + 1) * 128] = block
            terms[o] = dot_first(block, tokens[...]).astype(half)

    def expand(kind, maps, columns):
        total = jnp.zeros((x.shape[0], TILE), f32)
        for o in range(nz):
            total += jnp.dot(spread_low[kind, :, o * 128:(o + 1) * 128], maps[o, :, columns],
                             preferred_element_type=f32)
        return total.astype(half).astype(f32)

    hop(0, 1)
    dy_far.start()
    dy_near.start()
    acc[...] = jnp.zeros_like(acc)
    forward(0)
    near_first.start()
    forward(1)
    near_first.wait_recv()
    part[2] = (part[2].astype(f32) + near[0].astype(f32)).astype(half)
    far_copy.start()
    land(0, 1)
    hop(0, 2)
    forward(2)
    near_second.start()
    forward(3)
    land(0, 2)
    hop(0, 3)
    dy_far.wait_recv()
    dy_relay.start()
    backward(4)
    land(0, 3)
    hop(1, 1)
    low_start(0, x, g_down)
    dy_near.wait_recv()
    low_end(0, dy, t_up)
    reduce_hop(1, 3)
    backward(5)
    land(1, 1)
    hop(1, 2)
    reduce_land(1, 3)
    reduce_hop(1, 2)
    backward(6)
    land(1, 2)
    hop(1, 3)
    reduce_land(1, 2)
    reduce_hop(1, 1)
    dy_relay.wait_recv()
    backward(7)
    land(1, 3)
    low_start(1, dy, g_up)
    low_end(1, x, t_down)
    reduce_hop(0, 3)
    reduce_land(1, 1)
    reduce_end(1, grad_up)
    near_second.wait_recv()
    far_copy.wait_recv()

    def finish_forward(j, carry):
        columns = pl.ds(pl.multiple_of(j * TILE, TILE), TILE)
        base = part[0, :, columns].astype(f32) + near[1, :, columns].astype(f32)
        base = base + far[:, columns].astype(f32)
        layer[:, columns] = (base + expand(0, g_up, columns)).astype(half)
        return carry

    def finish_backward(j, carry):
        columns = pl.ds(pl.multiple_of(j * TILE, TILE), TILE)
        sens[:, columns] = (acc[:, columns] + expand(1, g_down, columns)).astype(half)
        return carry

    lax.fori_loop(0, tiles, finish_forward, 0)
    reduce_land(0, 3)
    reduce_hop(0, 2)
    lax.fori_loop(0, tiles, finish_backward, 0)
    reduce_land(0, 2)
    reduce_hop(0, 1)
    reduce_land(0, 1)
    reduce_end(0, grad_down)
    for kind in (0, 1):
        for t in (1, 2, 3):
            sent(kind, t)
            reduce_sent(kind, t)
        for k in (1, 2, 3):
            low_copy(kind, k).wait_send()
    for copy in (dy_far, dy_near, dy_relay, near_first, near_second, far_copy):
        copy.wait_send()


def fused_call(x, dy, mask, down, up, w):
    rows, width = x.shape
    block = down.shape[0]
    dma = pltpu.SemaphoreType.DMA
    vmem = pl.BlockSpec(memory_space=pltpu.VMEM)
    scratch = [
        pltpu.VMEM((4, block, width), half),
        pltpu.VMEM((4, block, width), half),
        pltpu.VMEM((4, block, width), half),
        pltpu.VMEM((4, block, width), half),
        pltpu.VMEM((2, 3, block, width), half),
        pltpu.VMEM((2, 3, block, width), half),
        pltpu.VMEM((4, rows, width), half),
        pltpu.VMEM((2, rows, width), half),
        pltpu.VMEM((rows, width), half),
        pltpu.VMEM((3, rows, width), half),
        pltpu.VMEM((rows, width), f32),
        pltpu.VMEM((2, rows, 128), f32),
        pltpu.VMEM((2, 3, rows, 128), f32),
        pltpu.VMEM((2, rows, 4 * block), half),
        pltpu.VMEM((2, w.shape[0], TILE), half),
        dma((2,)),
        dma((2, 2, 3)),
        dma((2, 2, 3)),
        dma((2, 2, 3)),
        dma((2, 2, 3)),
        dma((6,)),
        dma((6,)),
        dma((2, 3)),
        dma((2, 3)),
    ]
    return pl.pallas_call(
        fused_kernel,
        out_shape=[
            jax.ShapeDtypeStruct((rows, width), half),
            jax.ShapeDtypeStruct((rows, width), half),
            jax.ShapeDtypeStruct((block, width), f32),
            jax.ShapeDtypeStruct((block, width), f32),
        ],
        in_specs=[vmem] * 5 + [pl.BlockSpec(memory_space=pl.ANY)],
        out_specs=[vmem] * 4,
        scratch_shapes=scratch,
        compiler_params=pltpu.CompilerParams(
            collective_id=0, has_side_effects=True, vmem_limit_bytes=58 * 1024 * 1024
        ),
        cost_estimate=pl.CostEstimate(
            flops=4 * rows * width * 4 * width, bytes_accessed=80 * 2**20, transcendentals=0
        ),
    )(x, dy, mask, down, up, w)


def fits(n_tensor, n_adapter, block, width):
    return n_tensor == 4 and n_adapter == 4 and block == 128 and width % (2 * TILE) == 0


def make(n_tensor, n_adapter):
    def on_device(
        tokens,
        tenant,
        adapter_storage_rows,
        frozen_projection_weight,
        shrink_factor_matrices,
        expand_factor_matrices,
        shrink_running_mean,
        expand_running_mean,
        shrink_running_variance,
        expand_running_variance,
        output_gradient,
    ):
        count = adapter_storage_rows.shape[0]
        own, rank, width = shrink_factor_matrices.shape
        zi, ti = lax.axis_index("adapter"), lax.axis_index("tensor")
        def finish(layer_result, input_sensitivity, grad_down, grad_up):
            shape = shrink_factor_matrices.shape
            p_up, m_up, v_up = optimizer_advance(
                expand_factor_matrices,
                grad_up.reshape(shape),
                expand_running_mean,
                expand_running_variance,
            )
            p_down, m_down, v_down = optimizer_advance(
                shrink_factor_matrices,
                grad_down.reshape(shape),
                shrink_running_mean,
                shrink_running_variance,
            )
            return (layer_result, input_sensitivity, p_down, p_up, m_down, m_up, v_down, v_up)

        if fits(n_tensor, n_adapter, own * rank, width):
            labels = lax.broadcasted_iota(jnp.int32, (1, count), 1)
            stored = jnp.sum(
                jnp.where(tenant == labels, adapter_storage_rows[None, :], 0),
                axis=1,
                keepdims=True,
            )
            place = lax.broadcasted_iota(jnp.int32, (1, count * rank), 1) // rank
            mask = (stored == place).astype(f32)
            layer_result, input_sensitivity, grad_down, grad_up = fused_call(
                tokens,
                output_gradient,
                mask,
                shrink_factor_matrices.reshape(own * rank, width),
                expand_factor_matrices.reshape(own * rank, width),
                frozen_projection_weight,
            )
            return finish(layer_result, input_sensitivity, grad_down, grad_up)

        down_own = shrink_factor_matrices.reshape(own * rank, width).astype(half)
        up_own = expand_factor_matrices.reshape(own * rank, width).astype(half)

        labels = lax.broadcasted_iota(jnp.int32, (1, count), 1)
        stored = jnp.sum(
            jnp.where(tenant == labels, adapter_storage_rows[None, :], 0), axis=1, keepdims=True
        )
        place = lax.broadcasted_iota(jnp.int32, (1, count * rank), 1) // rank
        row_of = lax.rem(zi - place // own + n_adapter, n_adapter) * own + lax.rem(place, own)
        mask = stored == row_of

        def fold(values):
            values = jnp.where(mask, values, 0.0)
            return sum(values[:, a * rank : (a + 1) * rank] for a in range(count))

        def spread(low):
            return jnp.where(mask, jnp.tile(low, (1, count)), jnp.zeros((), low.dtype))

        def last(a, b):
            return lax.dot_general(a, b, (((1,), (1,)), ((), ())), preferred_element_type=f32)

        down_all, _, _ = chain_gather(down_own, n_adapter, zi)
        up_all, _, _ = chain_gather(up_own, n_adapter, zi)

        partial = jnp.dot(
            tokens, frozen_projection_weight, preferred_element_type=f32
        ).astype(half)
        base_out = tensor_scatter(partial, n_tensor, ti)
        dy_full = tensor_gather(output_gradient, n_tensor, ti)

        def blocks(terms):
            return list(terms.reshape(n_adapter, own * rank, width))

        low = tensor_sum(fold(last(tokens, down_all)), n_tensor)
        low = spread((adapter_scale * low).astype(half))
        terms_up = lax.dot_general(
            low, output_gradient, (((0,), (0,)), ((), ())), preferred_element_type=f32
        )
        grad_up = chain_scatter(blocks(terms_up), n_adapter)

        back_low = tensor_sum(fold(last(output_gradient, up_all)), n_tensor)
        back_low = spread((adapter_scale * back_low).astype(half))
        terms_down = lax.dot_general(
            back_low, tokens, (((0,), (0,)), ((), ())), preferred_element_type=f32
        )
        grad_down = chain_scatter(blocks(terms_down), n_adapter)

        delta = jnp.dot(low, up_all, preferred_element_type=f32).astype(half)
        back = jnp.dot(back_low, down_all, preferred_element_type=f32).astype(half)
        layer_result = (base_out + delta.astype(f32)).astype(half)
        base_back = last(dy_full, frozen_projection_weight)
        input_sensitivity = (base_back + back.astype(f32)).astype(half)

        return finish(layer_result, input_sensitivity, grad_down, grad_up)

    return on_device


def solution(mesh):
    rows = P(("groups", "adapter"), "tensor")
    maps = P(("groups", "adapter"), None, "tensor")
    return jax.shard_map(
        make(mesh.shape["tensor"], mesh.shape["adapter"]),
        mesh=mesh,
        in_specs=(rows, P(("groups", "adapter"), None), P("groups"), P("tensor", None))
        + (maps,) * 6
        + (rows,),
        out_specs=(rows, rows) + (maps,) * 6,
        check_vma=False,
    )
```

```python
import functools

import jax
import jax.numpy as jnp
from jax import lax
from jax.experimental import pallas as pl
from jax.experimental.pallas import tpu as pltpu
from jax.sharding import PartitionSpec as P

beta_one = 0.9
beta_two = 0.999
learn_rate = 0.01
adam_eps = 1e-08
adam_step = 10
adapter_scale = 2.0
f32 = jnp.float32
half = jnp.bfloat16


def optimizer_advance(param, grad, first, second):
    first_next = beta_one * first + (1.0 - beta_one) * grad
    second_next = beta_two * second + (1.0 - beta_two) * grad * grad
    fix_one = 1.0 - beta_one**adam_step
    fix_two = 1.0 - beta_two**adam_step
    param_next = param - learn_rate * (first_next / fix_one) / (
        jnp.sqrt(second_next / fix_two) + adam_eps
    )
    return (param_next, first_next, second_next)


def swap(value, size, bit):
    return lax.ppermute(value, "tensor", [(i, i ^ bit) for i in range(size)])


def bits_down(size):
    bit = size // 2
    while bit:
        yield bit
        bit //= 2


def tensor_gather(value, size, me):
    rows, width = value.shape
    held = value[:, None, :]
    for bit in bits_down(size):
        other = swap(held, size, bit)
        high = (me & bit) != 0
        held = jnp.stack(
            [jnp.where(high, other, held), jnp.where(high, held, other)], axis=2
        ).reshape(rows, -1, width)
    return held.reshape(rows, size * width)


def tensor_scatter(value, size, me):
    rows = value.shape[0]
    held = value.reshape(rows, size, -1)
    width = held.shape[2]
    bit = 1
    total = held
    while bit < size:
        pairs = total.reshape(rows, -1, 2, width)
        mine = ((me & bit) != 0).astype(jnp.int32)
        keep = lax.dynamic_index_in_dim(pairs, mine, 2, keepdims=False)
        give = lax.dynamic_index_in_dim(pairs, 1 - mine, 2, keepdims=False)
        other = swap(give.astype(half), size, bit)
        total = keep.astype(f32) + other.astype(f32)
        bit *= 2
    return total.reshape(rows, width)


def tensor_sum(value, size):
    if size == 4:
        a, b, c = (swap(value, size, k) for k in (1, 2, 3))
        return (value + a) + (b + c)
    bit = 1
    while bit < size:
        value = value + swap(value, size, bit)
        bit *= 2
    return value


def chain_gather(own, size, me, after=None):
    left, right = [own], [own]
    for t in range(1, size):
        left.append(
            lax.ppermute(left[-1], "adapter", [(i, i + 1) for i in range(t - 1, size - 1)])
        )
        right.append(
            lax.ppermute(right[-1], "adapter", [(i, i - 1) for i in range(1, size - t + 1)])
        )
    slots = [own] + [jnp.where(me >= t, left[t], right[size - t]) for t in range(1, size)]
    return jnp.concatenate(slots, axis=0), left, right


def chain_scatter(terms, size):
    from_left = from_right = None
    for d in range(size - 1, 0, -1):
        rightward, leftward = terms[size - d], terms[d]
        if from_left is not None:
            rightward = rightward + from_left.astype(f32)
            leftward = leftward + from_right.astype(f32)
        from_left = lax.ppermute(
            rightward.astype(half), "adapter", [(i, i + 1) for i in range(size - d)]
        )
        from_right = lax.ppermute(
            leftward.astype(half), "adapter", [(i, i - 1) for i in range(d, size)]
        )
    total = terms[0]
    if from_left is not None:
        total = total + from_left.astype(f32) + from_right.astype(f32)
    return total


TILE = 512
MESH = pl.DeviceIdType.MESH


def dot_last(a, b):
    return lax.dot_general(a, b, (((1,), (1,)), ((), ())), preferred_element_type=f32)


def dot_first(a, b):
    return lax.dot_general(a, b, (((0,), (0,)), ((), ())), preferred_element_type=f32)


def fused_kernel(
    per, x, dy, tenant, ids, down, up, w,
    layer, sens, grad_down, grad_up,
    g_down, g_up, t_down, t_up, r_down, r_up,
    part, near, far, dyg, acc, made, mask, lows, low_in, spread_low,
    wbuf, w_sem, z_send, z_recv, r_send, r_recv, y_send, y_recv, l_send, l_recv, out_sem,
):
    zi, ti = lax.axis_index("adapter"), lax.axis_index("tensor")
    nz = 4
    peers = [ti, ti + 1 - 2 * (ti % 2), (ti + 2) % 4, 3 - ti]
    width = x.shape[1]
    tiles = width // TILE

    def when(cond, fn):
        pl.when(cond)(fn)

    barrier = pltpu.get_barrier_semaphore()
    when(zi > 0, lambda: pl.semaphore_signal(
        barrier, inc=1, device_id={"adapter": zi - 1}, device_id_type=MESH))
    when(zi < nz - 1, lambda: pl.semaphore_signal(
        barrier, inc=1, device_id={"adapter": zi + 1}, device_id_type=MESH))
    for k in (1, 2, 3):
        pl.semaphore_signal(barrier, inc=1, device_id={"tensor": peers[k]}, device_id_type=MESH)
    g_down[zi] = down[...].astype(half)
    g_up[zi] = up[...].astype(half)

    order = [3, 2, 1, 0, 0, 1, 2, 3]

    def w_copy(s, j, slot):
        column = pl.multiple_of(peers[order[s]] * width + j * TILE, TILE)
        return pltpu.make_async_copy(w.at[:, pl.ds(column, TILE)], wbuf.at[slot], w_sem.at[slot])

    w_copy(0, 0, 0).start()
    inside = (zi > 0) & (zi < nz - 1)
    when(inside, lambda: pl.semaphore_wait(barrier, 5))
    when(jnp.logical_not(inside), lambda: pl.semaphore_wait(barrier, 4))

    def remote_z(src, dst, send, recv, direction):
        to = zi + 1 if direction == 0 else zi - 1
        return pltpu.make_async_remote_copy(
            src_ref=src, dst_ref=dst, send_sem=send, recv_sem=recv,
            device_id={"adapter": to}, device_id_type=MESH)

    cut = down.shape[0] // 2

    def rows_of(h):
        return pl.ds(h * cut, cut)

    def gather_copy(kind, t, h, direction, owner):
        g = (g_down, g_up)[kind]
        block = g.at[owner, rows_of(h)]
        return remote_z(block, block, z_send.at[kind, direction, t - 1, h],
                        z_recv.at[kind, direction, t - 1, h], direction)

    def may_right(t):
        return (zi < nz - 1) & (zi - t + 1 >= 0)

    def may_left(t):
        return (zi > 0) & (zi + t - 1 <= nz - 1)

    def hop(kind, t, h):
        when(may_right(t), lambda: gather_copy(kind, t, h, 0, zi - t + 1).start())
        when(may_left(t), lambda: gather_copy(kind, t, h, 1, zi + t - 1).start())

    def land(kind, t, h):
        when(zi - t >= 0, lambda: gather_copy(kind, t, h, 0, zi - t).wait_recv())
        when(zi + t <= nz - 1, lambda: gather_copy(kind, t, h, 1, zi + t).wait_recv())

    def sent(kind, t, h):
        when(may_right(t), lambda: gather_copy(kind, t, h, 0, zi - t + 1).wait_send())
        when(may_left(t), lambda: gather_copy(kind, t, h, 1, zi + t - 1).wait_send())

    def relay(kind, t):
        for h in (0, 1):
            land(kind, t, h)
            hop(kind, t + 1, h)

    def reduce_copy(kind, d, h, direction, owner):
        terms, arrived = ((t_down, r_down), (t_up, r_up))[kind]
        return remote_z(terms.at[owner, rows_of(h)], arrived.at[direction, d - 1, rows_of(h)],
                        r_send.at[kind, direction, d - 1, h],
                        r_recv.at[kind, direction, d - 1, h], direction)

    def reduce_hop(kind, d, h):
        terms, arrived = ((t_down, r_down), (t_up, r_up))[kind]

        def go(direction):
            owner = zi + d if direction == 0 else zi - d

            def fn():
                if d < nz - 1:
                    def add():
                        terms[owner, rows_of(h)] = (
                            terms[owner, rows_of(h)].astype(f32)
                            + arrived[direction, d, rows_of(h)].astype(f32)
                        ).astype(half)

                    when(zi > 0 if direction == 0 else zi < nz - 1, add)
                reduce_copy(kind, d, h, direction, owner).start()

            return fn

        when(zi + d <= nz - 1, go(0))
        when(zi - d >= 0, go(1))

    def reduce_land(kind, d, h):
        when((zi > 0) & (zi - 1 + d <= nz - 1),
             lambda: reduce_copy(kind, d, h, 0, 0).wait_recv())
        when((zi < nz - 1) & (zi + 1 - d >= 0),
             lambda: reduce_copy(kind, d, h, 1, 0).wait_recv())

    def reduce_sent(kind, d, h):
        when(zi + d <= nz - 1, lambda: reduce_copy(kind, d, h, 0, zi + d).wait_send())
        when(zi - d >= 0, lambda: reduce_copy(kind, d, h, 1, zi - d).wait_send())

    def reduce_relay(kind, d):
        for h in (0, 1):
            reduce_land(kind, d, h)
            reduce_hop(kind, d - 1, h)

    def reduce_end(kind, out):
        terms, arrived = ((t_down, r_down), (t_up, r_up))[kind]
        out[...] = terms[zi].astype(f32)

        def add(direction):
            def fn():
                out[...] += arrived[direction, 0].astype(f32)
            return fn

        when(zi > 0, add(0))
        when(zi < nz - 1, add(1))

    def remote_y(src, dst, n, k):
        return pltpu.make_async_remote_copy(
            src_ref=src, dst_ref=dst, send_sem=y_send.at[n], recv_sem=y_recv.at[n],
            device_id={"tensor": peers[k]}, device_id_type=MESH)

    dy_far = remote_y(dy, dyg.at[1], 0, 2)
    dy_near = remote_y(dy, dyg.at[0], 1, 1)
    dy_relay = remote_y(dyg.at[1], dyg.at[2], 2, 1)
    near_first = remote_y(part.at[3], near.at[0], 3, 1)
    near_second = remote_y(part.at[1], near.at[1], 4, 1)
    far_copy = remote_y(part.at[2], far, 5, 2)

    def stream(s, use):
        def step(j, carry):
            slot = lax.rem(j, 2)
            w_copy(s, j, slot).wait()

            @pl.when(j < tiles - 1)
            def _():
                w_copy(s, j + 1, 1 - slot).start()

            if s + 1 < len(order):
                @pl.when(j == tiles - 1)
                def _():
                    w_copy(s + 1, 0, 1 - slot).start()

            use(pl.ds(pl.multiple_of(j * TILE, TILE), TILE), wbuf.at[slot])
            return carry

        lax.fori_loop(0, tiles, step, 0)

    def forward(s):
        def use(columns, tile):
            part[order[s], :, columns] = jnp.dot(
                x[...], tile[...], preferred_element_type=f32
            ).astype(half)
        stream(s, use)

    def backward(s):
        k = order[s]
        source = dy if k == 0 else dyg.at[k - 1]

        def use(columns, tile):
            acc[...] += dot_last(source[:, columns], tile[...])
        stream(s, use)

    def low_start(kind, tokens, maps):
        total = jnp.zeros((x.shape[0], 128), f32)
        for o in range(nz):
            product = dot_last(tokens[...], maps[o])
            total += jnp.where(mask[:, o * 128:(o + 1) * 128] > 0.5, product, 0.0)
        lows[kind] = total
        for k in (1, 2, 3):
            low_copy(kind, k).start()

    def low_copy(kind, k):
        return pltpu.make_async_remote_copy(
            src_ref=lows.at[kind], dst_ref=low_in.at[kind, k - 1],
            send_sem=l_send.at[kind, k - 1], recv_sem=l_recv.at[kind, k - 1],
            device_id={"tensor": peers[k]}, device_id_type=MESH)

    def low_end(kind, tokens, terms):
        for k in (1, 2, 3):
            low_copy(kind, k).wait_recv()
        total = (lows[kind] + low_in[kind, 0]) + (low_in[kind, 1] + low_in[kind, 2])
        value = adapter_scale * total
        for o in range(nz):
            block = jnp.where(mask[:, o * 128:(o + 1) * 128] > 0.5, value, 0.0).astype(half)
            spread_low[kind, :, o * 128:(o + 1) * 128] = block
            terms[o] = dot_first(block, tokens[...]).astype(half)

    def expand(kind, maps, columns):
        total = jnp.zeros((x.shape[0], TILE), f32)
        for o in range(nz):
            total += jnp.dot(spread_low[kind, :, o * 128:(o + 1) * 128], maps[o, :, columns],
                             preferred_element_type=f32)
        return total.astype(half).astype(f32)

    hop(0, 1, 0)
    hop(0, 1, 1)
    dy_far.start()
    dy_near.start()
    acc[...] = jnp.zeros_like(acc)
    lanes = lax.broadcasted_iota(jnp.int32, (1, ids.shape[1]), 1)
    stored = jnp.sum(jnp.where(tenant[...] == lanes, ids[...], 0.0), axis=1, keepdims=True)
    places = (lax.broadcasted_iota(jnp.int32, (1, nz * 128), 1) // (128 // per)).astype(f32)
    mask[...] = jnp.where(stored == places, 1.0, 0.0)
    forward(0)
    near_first.start()
    forward(1)
    near_first.wait_recv()
    part[2] = (part[2].astype(f32) + near[0].astype(f32)).astype(half)
    far_copy.start()
    relay(0, 1)
    forward(2)
    near_second.start()
    forward(3)
    relay(0, 2)
    hop(1, 1, 0)
    dy_far.wait_recv()
    dy_relay.start()
    backward(4)
    land(0, 3, 0)
    land(0, 3, 1)
    hop(1, 1, 1)
    low_start(0, x, g_down)
    dy_near.wait_recv()
    low_end(0, dy, t_up)
    reduce_hop(1, 3, 0)
    reduce_hop(1, 3, 1)
    backward(5)
    relay(1, 1)
    reduce_relay(1, 3)
    backward(6)
    relay(1, 2)
    reduce_relay(1, 2)
    dy_relay.wait_recv()
    backward(7)
    land(1, 3, 0)
    land(1, 3, 1)
    low_start(1, dy, g_up)
    low_end(1, x, t_down)
    reduce_hop(0, 3, 0)
    reduce_hop(0, 3, 1)
    near_second.wait_recv()
    far_copy.wait_recv()

    def finish_forward(j, carry):
        columns = pl.ds(pl.multiple_of(j * TILE, TILE), TILE)
        base = part[0, :, columns].astype(f32) + near[1, :, columns].astype(f32)
        base = base + far[:, columns].astype(f32)
        made[:, columns] = base + expand(0, g_up, columns)
        return carry

    def finish_backward(j, carry):
        columns = pl.ds(pl.multiple_of(j * TILE, TILE), TILE)
        acc[:, columns] += expand(1, g_down, columns)
        return carry

    lax.fori_loop(0, tiles, finish_forward, 0)
    layer_out = pltpu.make_async_copy(made, layer, out_sem.at[0])
    layer_out.start()
    reduce_relay(0, 3)
    lax.fori_loop(0, tiles, finish_backward, 0)
    sens_out = pltpu.make_async_copy(acc, sens, out_sem.at[1])
    sens_out.start()
    reduce_land(1, 1, 0)
    reduce_land(1, 1, 1)
    reduce_end(1, grad_up)
    reduce_relay(0, 2)
    reduce_land(0, 1, 0)
    reduce_land(0, 1, 1)
    reduce_end(0, grad_down)
    layer_out.wait()
    sens_out.wait()
    for kind in (0, 1):
        for t in (1, 2, 3):
            for h in (0, 1):
                sent(kind, t, h)
                reduce_sent(kind, t, h)
        for k in (1, 2, 3):
            low_copy(kind, k).wait_send()
    for copy in (dy_far, dy_near, dy_relay, near_first, near_second, far_copy):
        copy.wait_send()


def fused_call(x, dy, tenant, ids, down, up, w):
    rows, width = x.shape
    block = down.shape[0]
    per = ids.shape[1] // 4
    dma = pltpu.SemaphoreType.DMA
    vmem = pl.BlockSpec(memory_space=pltpu.VMEM)
    scratch = [
        pltpu.VMEM((4, block, width), half),
        pltpu.VMEM((4, block, width), half),
        pltpu.VMEM((4, block, width), half),
        pltpu.VMEM((4, block, width), half),
        pltpu.VMEM((2, 3, block, width), half),
        pltpu.VMEM((2, 3, block, width), half),
        pltpu.VMEM((4, rows, width), half),
        pltpu.VMEM((2, rows, width), half),
        pltpu.VMEM((rows, width), half),
        pltpu.VMEM((3, rows, width), half),
        pltpu.VMEM((rows, width), f32),
        pltpu.VMEM((rows, width), f32),
        pltpu.VMEM((rows, 4 * block), f32),
        pltpu.VMEM((2, rows, 128), f32),
        pltpu.VMEM((2, 3, rows, 128), f32),
        pltpu.VMEM((2, rows, 4 * block), half),
        pltpu.VMEM((2, w.shape[0], TILE), half),
        dma((2,)),
        dma((2, 2, 3, 2)),
        dma((2, 2, 3, 2)),
        dma((2, 2, 3, 2)),
        dma((2, 2, 3, 2)),
        dma((6,)),
        dma((6,)),
        dma((2, 3)),
        dma((2, 3)),
        dma((2,)),
    ]
    return pl.pallas_call(
        functools.partial(fused_kernel, per),
        out_shape=[
            jax.ShapeDtypeStruct((rows, width), f32),
            jax.ShapeDtypeStruct((rows, width), f32),
            jax.ShapeDtypeStruct((block, width), f32),
            jax.ShapeDtypeStruct((block, width), f32),
        ],
        in_specs=[vmem] * 6 + [pl.BlockSpec(memory_space=pl.ANY)],
        out_specs=[pl.BlockSpec(memory_space=pl.ANY)] * 2 + [vmem] * 2,
        scratch_shapes=scratch,
        compiler_params=pltpu.CompilerParams(
            collective_id=0, has_side_effects=True, vmem_limit_bytes=58 * 1024 * 1024
        ),
        cost_estimate=pl.CostEstimate(
            flops=4 * rows * width * 4 * width, bytes_accessed=80 * 2**20, transcendentals=0
        ),
    )(x, dy, tenant, ids, down, up, w)


def fits(n_tensor, n_adapter, block, width):
    return n_tensor == 4 and n_adapter == 4 and block == 128 and width % (2 * TILE) == 0


def make(n_tensor, n_adapter):
    def on_device(
        tokens,
        tenant,
        adapter_storage_rows,
        frozen_projection_weight,
        shrink_factor_matrices,
        expand_factor_matrices,
        shrink_running_mean,
        expand_running_mean,
        shrink_running_variance,
        expand_running_variance,
        output_gradient,
    ):
        count = adapter_storage_rows.shape[0]
        own, rank, width = shrink_factor_matrices.shape
        zi, ti = lax.axis_index("adapter"), lax.axis_index("tensor")
        def finish(layer_result, input_sensitivity, grad_down, grad_up):
            shape = shrink_factor_matrices.shape
            p_up, m_up, v_up = optimizer_advance(
                expand_factor_matrices,
                grad_up.reshape(shape),
                expand_running_mean,
                expand_running_variance,
            )
            p_down, m_down, v_down = optimizer_advance(
                shrink_factor_matrices,
                grad_down.reshape(shape),
                shrink_running_mean,
                shrink_running_variance,
            )
            return (layer_result, input_sensitivity, p_down, p_up, m_down, m_up, v_down, v_up)

        if fits(n_tensor, n_adapter, own * rank, width):
            layer_result, input_sensitivity, grad_down, grad_up = fused_call(
                tokens,
                output_gradient,
                tenant,
                adapter_storage_rows.astype(f32).reshape(1, count),
                shrink_factor_matrices.reshape(own * rank, width),
                expand_factor_matrices.reshape(own * rank, width),
                frozen_projection_weight,
            )
            return finish(
                layer_result.astype(half), input_sensitivity.astype(half), grad_down, grad_up
            )

        down_own = shrink_factor_matrices.reshape(own * rank, width).astype(half)
        up_own = expand_factor_matrices.reshape(own * rank, width).astype(half)

        labels = lax.broadcasted_iota(jnp.int32, (1, count), 1)
        stored = jnp.sum(
            jnp.where(tenant == labels, adapter_storage_rows[None, :], 0), axis=1, keepdims=True
        )
        place = lax.broadcasted_iota(jnp.int32, (1, count * rank), 1) // rank
        row_of = lax.rem(zi - place // own + n_adapter, n_adapter) * own + lax.rem(place, own)
        mask = stored == row_of

        def fold(values):
            values = jnp.where(mask, values, 0.0)
            return sum(values[:, a * rank : (a + 1) * rank] for a in range(count))

        def spread(low):
            return jnp.where(mask, jnp.tile(low, (1, count)), jnp.zeros((), low.dtype))

        def last(a, b):
            return lax.dot_general(a, b, (((1,), (1,)), ((), ())), preferred_element_type=f32)

        down_all, _, _ = chain_gather(down_own, n_adapter, zi)
        up_all, _, _ = chain_gather(up_own, n_adapter, zi)

        partial = jnp.dot(
            tokens, frozen_projection_weight, preferred_element_type=f32
        ).astype(half)
        base_out = tensor_scatter(partial, n_tensor, ti)
        dy_full = tensor_gather(output_gradient, n_tensor, ti)

        def blocks(terms):
            return list(terms.reshape(n_adapter, own * rank, width))

        low = tensor_sum(fold(last(tokens, down_all)), n_tensor)
        low = spread((adapter_scale * low).astype(half))
        terms_up = lax.dot_general(
            low, output_gradient, (((0,), (0,)), ((), ())), preferred_element_type=f32
        )
        grad_up = chain_scatter(blocks(terms_up), n_adapter)

        back_low = tensor_sum(fold(last(output_gradient, up_all)), n_tensor)
        back_low = spread((adapter_scale * back_low).astype(half))
        terms_down = lax.dot_general(
            back_low, tokens, (((0,), (0,)), ((), ())), preferred_element_type=f32
        )
        grad_down = chain_scatter(blocks(terms_down), n_adapter)

        delta = jnp.dot(low, up_all, preferred_element_type=f32).astype(half)
        back = jnp.dot(back_low, down_all, preferred_element_type=f32).astype(half)
        layer_result = (base_out + delta.astype(f32)).astype(half)
        base_back = last(dy_full, frozen_projection_weight)
        input_sensitivity = (base_back + back.astype(f32)).astype(half)

        return finish(layer_result, input_sensitivity, grad_down, grad_up)

    return on_device


def solution(mesh):
    rows = P(("groups", "adapter"), "tensor")
    maps = P(("groups", "adapter"), None, "tensor")
    return jax.shard_map(
        make(mesh.shape["tensor"], mesh.shape["adapter"]),
        mesh=mesh,
        in_specs=(rows, P(("groups", "adapter"), None), P("groups"), P("tensor", None))
        + (maps,) * 6
        + (rows,),
        out_specs=(rows, rows) + (maps,) * 6,
        check_vma=False,
    )
```

```python
import functools

import jax
import jax.numpy as jnp
from jax import lax
from jax.experimental import pallas as pl
from jax.experimental.pallas import tpu as pltpu
from jax.sharding import PartitionSpec as P

beta_one = 0.9
beta_two = 0.999
learn_rate = 0.01
adam_eps = 1e-08
adam_step = 10
adapter_scale = 2.0
f32 = jnp.float32
half = jnp.bfloat16


def optimizer_advance(param, grad, first, second):
    first_next = beta_one * first + (1.0 - beta_one) * grad
    second_next = beta_two * second + (1.0 - beta_two) * grad * grad
    fix_one = 1.0 - beta_one**adam_step
    fix_two = 1.0 - beta_two**adam_step
    param_next = param - learn_rate * (first_next / fix_one) / (
        jnp.sqrt(second_next / fix_two) + adam_eps
    )
    return (param_next, first_next, second_next)


def swap(value, size, bit):
    return lax.ppermute(value, "tensor", [(i, i ^ bit) for i in range(size)])


def bits_down(size):
    bit = size // 2
    while bit:
        yield bit
        bit //= 2


def tensor_gather(value, size, me):
    rows, width = value.shape
    held = value[:, None, :]
    for bit in bits_down(size):
        other = swap(held, size, bit)
        high = (me & bit) != 0
        held = jnp.stack(
            [jnp.where(high, other, held), jnp.where(high, held, other)], axis=2
        ).reshape(rows, -1, width)
    return held.reshape(rows, size * width)


def tensor_scatter(value, size, me):
    rows = value.shape[0]
    held = value.reshape(rows, size, -1)
    width = held.shape[2]
    bit = 1
    total = held
    while bit < size:
        pairs = total.reshape(rows, -1, 2, width)
        mine = ((me & bit) != 0).astype(jnp.int32)
        keep = lax.dynamic_index_in_dim(pairs, mine, 2, keepdims=False)
        give = lax.dynamic_index_in_dim(pairs, 1 - mine, 2, keepdims=False)
        other = swap(give.astype(half), size, bit)
        total = keep.astype(f32) + other.astype(f32)
        bit *= 2
    return total.reshape(rows, width)


def tensor_sum(value, size):
    if size == 4:
        a, b, c = (swap(value, size, k) for k in (1, 2, 3))
        return (value + a) + (b + c)
    bit = 1
    while bit < size:
        value = value + swap(value, size, bit)
        bit *= 2
    return value


def chain_gather(own, size, me, after=None):
    left, right = [own], [own]
    for t in range(1, size):
        left.append(
            lax.ppermute(left[-1], "adapter", [(i, i + 1) for i in range(t - 1, size - 1)])
        )
        right.append(
            lax.ppermute(right[-1], "adapter", [(i, i - 1) for i in range(1, size - t + 1)])
        )
    slots = [own] + [jnp.where(me >= t, left[t], right[size - t]) for t in range(1, size)]
    return jnp.concatenate(slots, axis=0), left, right


def chain_scatter(terms, size):
    from_left = from_right = None
    for d in range(size - 1, 0, -1):
        rightward, leftward = terms[size - d], terms[d]
        if from_left is not None:
            rightward = rightward + from_left.astype(f32)
            leftward = leftward + from_right.astype(f32)
        from_left = lax.ppermute(
            rightward.astype(half), "adapter", [(i, i + 1) for i in range(size - d)]
        )
        from_right = lax.ppermute(
            leftward.astype(half), "adapter", [(i, i - 1) for i in range(d, size)]
        )
    total = terms[0]
    if from_left is not None:
        total = total + from_left.astype(f32) + from_right.astype(f32)
    return total


TILE = 512
MESH = pl.DeviceIdType.MESH


def dot_last(a, b):
    return lax.dot_general(a, b, (((1,), (1,)), ((), ())), preferred_element_type=f32)


def dot_first(a, b):
    return lax.dot_general(a, b, (((0,), (0,)), ((), ())), preferred_element_type=f32)


def fused_kernel(
    per, x, dy, tenant, ids, down, up, w,
    layer, sens, grad_down, grad_up,
    g_down, g_up, t_down, t_up, r_down, r_up,
    part, near, far, dyg, acc, made, mask, lows, low_in, spread_low,
    wbuf, w_sem, z_send, z_recv, r_send, r_recv, y_send, y_recv, l_send, l_recv, out_sem,
):
    zi, ti = lax.axis_index("adapter"), lax.axis_index("tensor")
    nz = 4
    peers = [ti, ti + 1 - 2 * (ti % 2), (ti + 2) % 4, 3 - ti]
    width = x.shape[1]
    tiles = width // TILE

    def when(cond, fn):
        pl.when(cond)(fn)

    barrier = pltpu.get_barrier_semaphore()
    when(zi > 0, lambda: pl.semaphore_signal(
        barrier, inc=1, device_id={"adapter": zi - 1}, device_id_type=MESH))
    when(zi < nz - 1, lambda: pl.semaphore_signal(
        barrier, inc=1, device_id={"adapter": zi + 1}, device_id_type=MESH))
    for k in (1, 2, 3):
        pl.semaphore_signal(barrier, inc=1, device_id={"tensor": peers[k]}, device_id_type=MESH)
    g_down[zi] = down[...].astype(half)

    order = [3, 2, 1, 0, 0, 1, 2, 3]

    def w_copy(s, j, slot):
        column = pl.multiple_of(peers[order[s]] * width + j * TILE, TILE)
        return pltpu.make_async_copy(w.at[:, pl.ds(column, TILE)], wbuf.at[slot], w_sem.at[slot])

    w_copy(0, 0, 0).start()
    inside = (zi > 0) & (zi < nz - 1)
    when(inside, lambda: pl.semaphore_wait(barrier, 5))
    when(jnp.logical_not(inside), lambda: pl.semaphore_wait(barrier, 4))

    def remote_z(src, dst, send, recv, direction):
        to = zi + 1 if direction == 0 else zi - 1
        return pltpu.make_async_remote_copy(
            src_ref=src, dst_ref=dst, send_sem=send, recv_sem=recv,
            device_id={"adapter": to}, device_id_type=MESH)

    cut = down.shape[0] // 2

    def rows_of(h):
        return pl.ds(h * cut, cut)

    def gather_copy(kind, t, h, direction, owner):
        g = (g_down, g_up)[kind]
        block = g.at[owner, rows_of(h)]
        return remote_z(block, block, z_send.at[kind, direction, t - 1, h],
                        z_recv.at[kind, direction, t - 1, h], direction)

    def may_right(t):
        return (zi < nz - 1) & (zi - t + 1 >= 0)

    def may_left(t):
        return (zi > 0) & (zi + t - 1 <= nz - 1)

    def hop(kind, t, h):
        when(may_right(t), lambda: gather_copy(kind, t, h, 0, zi - t + 1).start())
        when(may_left(t), lambda: gather_copy(kind, t, h, 1, zi + t - 1).start())

    def land(kind, t, h):
        when(zi - t >= 0, lambda: gather_copy(kind, t, h, 0, zi - t).wait_recv())
        when(zi + t <= nz - 1, lambda: gather_copy(kind, t, h, 1, zi + t).wait_recv())

    def sent(kind, t, h):
        when(may_right(t), lambda: gather_copy(kind, t, h, 0, zi - t + 1).wait_send())
        when(may_left(t), lambda: gather_copy(kind, t, h, 1, zi + t - 1).wait_send())

    def relay(kind, t):
        for h in (0, 1):
            land(kind, t, h)
            hop(kind, t + 1, h)

    def reduce_copy(kind, d, h, direction, owner):
        terms, arrived = ((t_down, r_down), (t_up, r_up))[kind]
        return remote_z(terms.at[owner, rows_of(h)], arrived.at[direction, d - 1, rows_of(h)],
                        r_send.at[kind, direction, d - 1, h],
                        r_recv.at[kind, direction, d - 1, h], direction)

    def reduce_hop(kind, d, h):
        terms, arrived = ((t_down, r_down), (t_up, r_up))[kind]

        def go(direction):
            owner = zi + d if direction == 0 else zi - d

            def fn():
                if d < nz - 1:
                    def add():
                        terms[owner, rows_of(h)] = (
                            terms[owner, rows_of(h)].astype(f32)
                            + arrived[direction, d, rows_of(h)].astype(f32)
                        ).astype(half)

                    when(zi > 0 if direction == 0 else zi < nz - 1, add)
                reduce_copy(kind, d, h, direction, owner).start()

            return fn

        when(zi + d <= nz - 1, go(0))
        when(zi - d >= 0, go(1))

    def reduce_land(kind, d, h):
        when((zi > 0) & (zi - 1 + d <= nz - 1),
             lambda: reduce_copy(kind, d, h, 0, 0).wait_recv())
        when((zi < nz - 1) & (zi + 1 - d >= 0),
             lambda: reduce_copy(kind, d, h, 1, 0).wait_recv())

    def reduce_sent(kind, d, h):
        when(zi + d <= nz - 1, lambda: reduce_copy(kind, d, h, 0, zi + d).wait_send())
        when(zi - d >= 0, lambda: reduce_copy(kind, d, h, 1, zi - d).wait_send())

    def reduce_relay(kind, d):
        for h in (0, 1):
            reduce_land(kind, d, h)
            reduce_hop(kind, d - 1, h)

    def reduce_end(kind, out):
        terms, arrived = ((t_down, r_down), (t_up, r_up))[kind]
        out[...] = terms[zi].astype(f32)

        def add(direction):
            def fn():
                out[...] += arrived[direction, 0].astype(f32)
            return fn

        when(zi > 0, add(0))
        when(zi < nz - 1, add(1))

    def remote_y(src, dst, n, k):
        return pltpu.make_async_remote_copy(
            src_ref=src, dst_ref=dst, send_sem=y_send.at[n], recv_sem=y_recv.at[n],
            device_id={"tensor": peers[k]}, device_id_type=MESH)

    dy_far = remote_y(dy, dyg.at[1], 0, 2)
    dy_near = remote_y(dy, dyg.at[0], 1, 1)
    dy_relay = remote_y(dyg.at[1], dyg.at[2], 2, 1)
    near_first = remote_y(part.at[3], near.at[0], 3, 1)
    near_second = remote_y(part.at[1], near.at[1], 4, 1)
    far_copy = remote_y(part.at[2], far, 5, 2)

    def stream(s, use):
        def step(j, carry):
            slot = lax.rem(j, 2)
            w_copy(s, j, slot).wait()

            @pl.when(j < tiles - 1)
            def _():
                w_copy(s, j + 1, 1 - slot).start()

            if s + 1 < len(order):
                @pl.when(j == tiles - 1)
                def _():
                    w_copy(s + 1, 0, 1 - slot).start()

            use(pl.ds(pl.multiple_of(j * TILE, TILE), TILE), wbuf.at[slot])
            return carry

        lax.fori_loop(0, tiles, step, 0)

    def forward(s):
        def use(columns, tile):
            part[order[s], :, columns] = jnp.dot(
                x[...], tile[...], preferred_element_type=f32
            ).astype(half)
        stream(s, use)

    def backward(s):
        k = order[s]
        source = dy if k == 0 else dyg.at[k - 1]

        def use(columns, tile):
            acc[...] += dot_last(source[:, columns], tile[...])
        stream(s, use)

    def low_start(kind, tokens, maps):
        total = jnp.zeros((x.shape[0], 128), f32)
        for o in range(nz):
            product = dot_last(tokens[...], maps[o])
            total += jnp.where(mask[:, o * 128:(o + 1) * 128] > 0.5, product, 0.0)
        lows[kind] = total
        for k in (1, 2, 3):
            low_copy(kind, k).start()

    def low_copy(kind, k):
        return pltpu.make_async_remote_copy(
            src_ref=lows.at[kind], dst_ref=low_in.at[kind, k - 1],
            send_sem=l_send.at[kind, k - 1], recv_sem=l_recv.at[kind, k - 1],
            device_id={"tensor": peers[k]}, device_id_type=MESH)

    def low_end(kind, tokens, terms):
        for k in (1, 2, 3):
            low_copy(kind, k).wait_recv()
        total = (lows[kind] + low_in[kind, 0]) + (low_in[kind, 1] + low_in[kind, 2])
        value = adapter_scale * total
        for o in range(nz):
            block = jnp.where(mask[:, o * 128:(o + 1) * 128] > 0.5, value, 0.0).astype(half)
            spread_low[kind, :, o * 128:(o + 1) * 128] = block
            terms[o] = dot_first(block, tokens[...]).astype(half)

    def expand(kind, maps, columns):
        total = jnp.zeros((x.shape[0], TILE), f32)
        for o in range(nz):
            total += jnp.dot(spread_low[kind, :, o * 128:(o + 1) * 128], maps[o, :, columns],
                             preferred_element_type=f32)
        return total.astype(half).astype(f32)

    hop(0, 1, 0)
    hop(0, 1, 1)
    dy_far.start()
    dy_near.start()
    g_up[zi] = up[...].astype(half)
    acc[...] = jnp.zeros_like(acc)
    lanes = lax.broadcasted_iota(jnp.int32, (1, ids.shape[1]), 1)
    stored = jnp.sum(jnp.where(tenant[...] == lanes, ids[...], 0.0), axis=1, keepdims=True)
    places = (lax.broadcasted_iota(jnp.int32, (1, nz * 128), 1) // (128 // per)).astype(f32)
    mask[...] = jnp.where(stored == places, 1.0, 0.0)
    forward(0)
    near_first.start()
    forward(1)
    near_first.wait_recv()
    part[2] = (part[2].astype(f32) + near[0].astype(f32)).astype(half)
    far_copy.start()
    relay(0, 1)
    forward(2)
    near_second.start()
    forward(3)
    relay(0, 2)
    hop(1, 1, 0)
    hop(1, 1, 1)
    dy_far.wait_recv()
    dy_relay.start()
    backward(4)
    land(0, 3, 0)
    land(0, 3, 1)
    low_start(0, x, g_down)
    dy_near.wait_recv()
    low_end(0, dy, t_up)
    reduce_hop(1, 3, 0)
    reduce_hop(1, 3, 1)
    relay(1, 1)
    backward(5)
    reduce_relay(1, 3)
    backward(6)
    relay(1, 2)
    reduce_relay(1, 2)
    dy_relay.wait_recv()
    backward(7)
    land(1, 3, 0)
    land(1, 3, 1)
    low_start(1, dy, g_up)
    low_end(1, x, t_down)
    reduce_hop(0, 3, 0)
    reduce_hop(0, 3, 1)
    near_second.wait_recv()
    far_copy.wait_recv()

    def finish_forward(j, carry):
        columns = pl.ds(pl.multiple_of(j * TILE, TILE), TILE)
        base = part[0, :, columns].astype(f32) + near[1, :, columns].astype(f32)
        base = base + far[:, columns].astype(f32)
        made[:, columns] = base + expand(0, g_up, columns)
        return carry

    def finish_backward(j, carry):
        columns = pl.ds(pl.multiple_of(j * TILE, TILE), TILE)
        acc[:, columns] += expand(1, g_down, columns)
        return carry

    lax.fori_loop(0, tiles, finish_forward, 0)
    layer_out = pltpu.make_async_copy(made, layer, out_sem.at[0])
    layer_out.start()
    reduce_relay(0, 3)
    lax.fori_loop(0, tiles, finish_backward, 0)
    sens_out = pltpu.make_async_copy(acc, sens, out_sem.at[1])
    sens_out.start()
    reduce_land(1, 1, 0)
    reduce_land(1, 1, 1)
    reduce_end(1, grad_up)
    reduce_relay(0, 2)
    reduce_land(0, 1, 0)
    reduce_land(0, 1, 1)
    reduce_end(0, grad_down)
    layer_out.wait()
    sens_out.wait()
    for kind in (0, 1):
        for t in (1, 2, 3):
            for h in (0, 1):
                sent(kind, t, h)
                reduce_sent(kind, t, h)
        for k in (1, 2, 3):
            low_copy(kind, k).wait_send()
    for copy in (dy_far, dy_near, dy_relay, near_first, near_second, far_copy):
        copy.wait_send()


def fused_call(x, dy, tenant, ids, down, up, w):
    rows, width = x.shape
    block = down.shape[0]
    per = ids.shape[1] // 4
    dma = pltpu.SemaphoreType.DMA
    vmem = pl.BlockSpec(memory_space=pltpu.VMEM)
    scratch = [
        pltpu.VMEM((4, block, width), half),
        pltpu.VMEM((4, block, width), half),
        pltpu.VMEM((4, block, width), half),
        pltpu.VMEM((4, block, width), half),
        pltpu.VMEM((2, 3, block, width), half),
        pltpu.VMEM((2, 3, block, width), half),
        pltpu.VMEM((4, rows, width), half),
        pltpu.VMEM((2, rows, width), half),
        pltpu.VMEM((rows, width), half),
        pltpu.VMEM((3, rows, width), half),
        pltpu.VMEM((rows, width), f32),
        pltpu.VMEM((rows, width), f32),
        pltpu.VMEM((rows, 4 * block), f32),
        pltpu.VMEM((2, rows, 128), f32),
        pltpu.VMEM((2, 3, rows, 128), f32),
        pltpu.VMEM((2, rows, 4 * block), half),
        pltpu.VMEM((2, w.shape[0], TILE), half),
        dma((2,)),
        dma((2, 2, 3, 2)),
        dma((2, 2, 3, 2)),
        dma((2, 2, 3, 2)),
        dma((2, 2, 3, 2)),
        dma((6,)),
        dma((6,)),
        dma((2, 3)),
        dma((2, 3)),
        dma((2,)),
    ]
    return pl.pallas_call(
        functools.partial(fused_kernel, per),
        out_shape=[
            jax.ShapeDtypeStruct((rows, width), f32),
            jax.ShapeDtypeStruct((rows, width), f32),
            jax.ShapeDtypeStruct((block, width), f32),
            jax.ShapeDtypeStruct((block, width), f32),
        ],
        in_specs=[vmem] * 6 + [pl.BlockSpec(memory_space=pl.ANY)],
        out_specs=[pl.BlockSpec(memory_space=pl.ANY)] * 2 + [vmem] * 2,
        scratch_shapes=scratch,
        compiler_params=pltpu.CompilerParams(
            collective_id=0, has_side_effects=True, vmem_limit_bytes=58 * 1024 * 1024
        ),
        cost_estimate=pl.CostEstimate(
            flops=4 * rows * width * 4 * width, bytes_accessed=80 * 2**20, transcendentals=0
        ),
    )(x, dy, tenant, ids, down, up, w)


def fits(n_tensor, n_adapter, block, width):
    return n_tensor == 4 and n_adapter == 4 and block == 128 and width % (2 * TILE) == 0


def make(n_tensor, n_adapter):
    def on_device(
        tokens,
        tenant,
        adapter_storage_rows,
        frozen_projection_weight,
        shrink_factor_matrices,
        expand_factor_matrices,
        shrink_running_mean,
        expand_running_mean,
        shrink_running_variance,
        expand_running_variance,
        output_gradient,
    ):
        count = adapter_storage_rows.shape[0]
        own, rank, width = shrink_factor_matrices.shape
        zi, ti = lax.axis_index("adapter"), lax.axis_index("tensor")
        def finish(layer_result, input_sensitivity, grad_down, grad_up):
            shape = shrink_factor_matrices.shape
            p_up, m_up, v_up = optimizer_advance(
                expand_factor_matrices,
                grad_up.reshape(shape),
                expand_running_mean,
                expand_running_variance,
            )
            p_down, m_down, v_down = optimizer_advance(
                shrink_factor_matrices,
                grad_down.reshape(shape),
                shrink_running_mean,
                shrink_running_variance,
            )
            return (layer_result, input_sensitivity, p_down, p_up, m_down, m_up, v_down, v_up)

        if fits(n_tensor, n_adapter, own * rank, width):
            layer_result, input_sensitivity, grad_down, grad_up = fused_call(
                tokens,
                output_gradient,
                tenant,
                adapter_storage_rows.astype(f32).reshape(1, count),
                shrink_factor_matrices.reshape(own * rank, width),
                expand_factor_matrices.reshape(own * rank, width),
                frozen_projection_weight,
            )
            return finish(
                layer_result.astype(half), input_sensitivity.astype(half), grad_down, grad_up
            )

        down_own = shrink_factor_matrices.reshape(own * rank, width).astype(half)
        up_own = expand_factor_matrices.reshape(own * rank, width).astype(half)

        labels = lax.broadcasted_iota(jnp.int32, (1, count), 1)
        stored = jnp.sum(
            jnp.where(tenant == labels, adapter_storage_rows[None, :], 0), axis=1, keepdims=True
        )
        place = lax.broadcasted_iota(jnp.int32, (1, count * rank), 1) // rank
        row_of = lax.rem(zi - place // own + n_adapter, n_adapter) * own + lax.rem(place, own)
        mask = stored == row_of

        def fold(values):
            values = jnp.where(mask, values, 0.0)
            return sum(values[:, a * rank : (a + 1) * rank] for a in range(count))

        def spread(low):
            return jnp.where(mask, jnp.tile(low, (1, count)), jnp.zeros((), low.dtype))

        def last(a, b):
            return lax.dot_general(a, b, (((1,), (1,)), ((), ())), preferred_element_type=f32)

        down_all, _, _ = chain_gather(down_own, n_adapter, zi)
        up_all, _, _ = chain_gather(up_own, n_adapter, zi)

        partial = jnp.dot(
            tokens, frozen_projection_weight, preferred_element_type=f32
        ).astype(half)
        base_out = tensor_scatter(partial, n_tensor, ti)
        dy_full = tensor_gather(output_gradient, n_tensor, ti)

        def blocks(terms):
            return list(terms.reshape(n_adapter, own * rank, width))

        low = tensor_sum(fold(last(tokens, down_all)), n_tensor)
        low = spread((adapter_scale * low).astype(half))
        terms_up = lax.dot_general(
            low, output_gradient, (((0,), (0,)), ((), ())), preferred_element_type=f32
        )
        grad_up = chain_scatter(blocks(terms_up), n_adapter)

        back_low = tensor_sum(fold(last(output_gradient, up_all)), n_tensor)
        back_low = spread((adapter_scale * back_low).astype(half))
        terms_down = lax.dot_general(
            back_low, tokens, (((0,), (0,)), ((), ())), preferred_element_type=f32
        )
        grad_down = chain_scatter(blocks(terms_down), n_adapter)

        delta = jnp.dot(low, up_all, preferred_element_type=f32).astype(half)
        back = jnp.dot(back_low, down_all, preferred_element_type=f32).astype(half)
        layer_result = (base_out + delta.astype(f32)).astype(half)
        base_back = last(dy_full, frozen_projection_weight)
        input_sensitivity = (base_back + back.astype(f32)).astype(half)

        return finish(layer_result, input_sensitivity, grad_down, grad_up)

    return on_device


def solution(mesh):
    rows = P(("groups", "adapter"), "tensor")
    maps = P(("groups", "adapter"), None, "tensor")
    return jax.shard_map(
        make(mesh.shape["tensor"], mesh.shape["adapter"]),
        mesh=mesh,
        in_specs=(rows, P(("groups", "adapter"), None), P("groups"), P("tensor", None))
        + (maps,) * 6
        + (rows,),
        out_specs=(rows, rows) + (maps,) * 6,
        check_vma=False,
    )
```
